128 devices in a mesh: seq: 32 (over z, y, core), head: 4 (over x).
Axes of the slice: x: 4, y: 4, z: 4, core: 2. Of those that a mesh axis runs over, the one named last changes fastest.
Arguments:
- query_states: bfloat16 [8192, 1536], P('seq', 'head'), may hold values from -100 to 100
- key_states: bfloat16 [8192, 1536], P('seq', 'head'), may hold values from -4.1 to 4.1
- value_states: bfloat16 [8192, 1536], P('seq', 'head'), may hold values from -6 to 6
- out_weight: bfloat16 [1536, 1536], P('head'), may hold values from -0.15625 to 0.15625
- out_grad: bfloat16 [8192, 1536], P(('seq', 'head')), may hold values from -6 to 6
- placement: int32 [32], replicated, may hold values from 0 to 31, each once
- sink_ids: int32 [256], replicated, may hold values from 0 to 8191, as said below
- span_mask: int32 [32, 32], replicated, may hold values from 0 to 1, as said below
Outputs:
- mixed: bfloat16 [8192, 1536], P(('seq', 'head'))
- query_grad: bfloat16 [8192, 1536], P('seq', 'head')
- key_grad: bfloat16 [8192, 1536], P('seq', 'head')
- value_grad: bfloat16 [8192, 1536], P('seq', 'head')
The draws below stay inside these ranges and needn't reach their ends.
Inputs may be any that keep to these rules, and one draw needn't show every extreme that they name: `sink_ids`: 256 distinct row positions. The spans form contiguous runs of consecutive span numbers, starting with span 0; span_mask[c, e] is 1 when e lies in the run of c or in an earlier run, and 0 when e lies in a later run.
All inputs are finite; a program needn't handle non-finite values.
Results may differ from the reference program's by a relative error of at most 0.04.
Values may be sent and summed in bfloat16 or wider, within the bound.
A program may use at most 128 MiB of HBM per device.

```python
import jax
import jax.numpy as jnp
from jax import lax

HEADS = 12
HD = 128
D = 1536
TOK_DEV = 256
SINKS = 256
SPANS = 32
TOKENS = 8192
N_HEAD = 4


def shared_keys(key):
    return jnp.clip(jax.random.normal(key, (TOKENS, D), jnp.float32), -4.0, 4.0)


def draw_key_states(key, part):
    base = shared_keys(key)
    return base.astype(jnp.bfloat16)


def draw_query_states(key, part):
    key = jax.random.fold_in(key, 2)
    fresh = jnp.clip(jax.random.normal(key, (TOKENS, D), jnp.float32), -4.0, 4.0)
    return fresh.astype(jnp.bfloat16)


def draw_sink_ids(key, part):
    key = jax.random.fold_in(key, 3)
    return jax.random.permutation(key, TOKENS)[:SINKS].astype(jnp.int32)


def draw_span_mask(key, part):
    key = jax.random.fold_in(key, 5)
    steps_up = jax.random.randint(key, (SPANS,), 0, 2).astype(jnp.int32)
    first = jnp.arange(SPANS, dtype=jnp.int32) == 0
    steps_up = jnp.where(first, jnp.zeros_like(steps_up), steps_up)
    run_of = jnp.cumsum(steps_up).astype(jnp.int32)
    return (run_of[None, :] <= run_of[:, None]).astype(jnp.int32)


def level_of(rng, shape, split, smallest, high):
    def one(dim, blocks):
        draws = jax.random.uniform(jax.random.fold_in(jax.random.fold_in(rng, 6), dim), (blocks,), jnp.float32, smallest / len(split), high / len(split))
        return jnp.repeat(jnp.exp(draws), shape[dim] // blocks).reshape((-1,) + (1,) * (len(shape) - dim - 1))

    loudness = one(*split[0])
    for cut in split[1:]:
        loudness = loudness * one(*cut)
    return loudness


def scatter_about(own_key, dims, width, limit, shards=(), kind=jnp.bfloat16):
    array = jax.random.normal(own_key, dims, jnp.float32) * width
    if len(shards) > 0:
        array = level_of(own_key, dims, shards, -0.22, 0.18) * array
    return jnp.clip(array, min=-limit, max=limit).astype(kind)


def setup_inputs(seed: int = 0) -> dict:
    splits = jax.random.split(jax.random.key(seed), 9)
    query_states = draw_query_states(jax.random.fold_in(splits[8], 71), 0)
    key_states = draw_key_states(jax.random.fold_in(splits[8], 71), 0)
    value_states = scatter_about(splits[2], (TOKENS, D), 1.0, 6.0, ((0, 32), (1, 4)))
    out_weight = scatter_about(splits[3], (D, D), D ** -0.5, 0.15625, ((0, 4),))
    out_grad = scatter_about(splits[4], (TOKENS, D), 1.0, 6.0, ((0, 128),))
    placement = jax.random.permutation(splits[5], SPANS).astype(jnp.int32)
    sink_ids = draw_sink_ids(jax.random.fold_in(splits[8], 71), 0)
    span_mask = draw_span_mask(jax.random.fold_in(splits[8], 71), 0)
    return dict(query_states=query_states, key_states=key_states, value_states=value_states, out_weight=out_weight, out_grad=out_grad, placement=placement, sink_ids=sink_ids, span_mask=span_mask)


def rounded(values):
    return lax.optimization_barrier(values.astype(jnp.bfloat16)).astype(jnp.float32)


def allowed_keys(block, placement, sink_ids, span_mask):
    key_block = jnp.arange(TOKENS, dtype=jnp.int32) // TOK_DEV
    is_sink = jnp.zeros((TOKENS,), jnp.bool_).at[sink_ids].set(True)
    mask_row = span_mask[placement[block]]
    return (mask_row[placement[key_block]] == 1) | is_sink


def reference(query_states, key_states, value_states, out_weight, out_grad, placement, sink_ids, span_mask):
    scale = HD ** -0.5
    queries = query_states.astype(jnp.float32).reshape(SPANS, TOK_DEV, HEADS, HD)
    keys_all = key_states.astype(jnp.float32).reshape(TOKENS, HEADS, HD)
    values_all = value_states.astype(jnp.float32).reshape(TOKENS, HEADS, HD)
    blocks = jnp.arange(SPANS, dtype=jnp.int32)

    def forward(block):
        scores = jnp.einsum('qhd,khd->qhk', queries[block], keys_all) * scale
        allow = allowed_keys(block, placement, sink_ids, span_mask)
        scores = jnp.where(allow[None, None, :], scores, -jnp.inf)
        top = jnp.max(scores, axis=-1)
        weights = jnp.exp(scores - top[..., None])
        total = jnp.sum(weights, axis=-1)
        summed = jnp.einsum('qhk,khd->qhd', rounded(weights), values_all)
        attn_block = (summed / total[..., None]).astype(jnp.bfloat16).reshape(TOK_DEV, D)
        return attn_block, top + jnp.log(total)

    attn, log_total = lax.map(forward, blocks)
    attn = attn.reshape(TOKENS, D)
    group_width = D // N_HEAD
    mixed_sum = jnp.zeros((TOKENS, D), jnp.float32)
    for group in range(N_HEAD):
        lower = group * group_width
        partial_term = jnp.dot(attn[:, lower:lower + group_width], out_weight[lower:lower + group_width, :],
                               preferred_element_type=jnp.float32)
        mixed_sum = mixed_sum + rounded(partial_term)
    mixed = mixed_sum.astype(jnp.bfloat16)
    d_attn = lax.dot_general(out_grad, out_weight, (((1,), (1,)), ((), ())), preferred_element_type=jnp.float32).astype(jnp.bfloat16)
    grad_heads = d_attn.astype(jnp.float32).reshape(SPANS, TOK_DEV, HEADS, HD)
    delta = jnp.sum(grad_heads * attn.astype(jnp.float32).reshape(SPANS, TOK_DEV, HEADS, HD), axis=-1)

    def backward(carry, block):
        key_acc, value_acc = carry
        scores = jnp.einsum('qhd,khd->qhk', queries[block], keys_all) * scale
        allow = allowed_keys(block, placement, sink_ids, span_mask)
        probs = jnp.where(allow[None, None, :], jnp.exp(scores - log_total[block][..., None]), 0.0)
        dots = jnp.einsum('qhd,khd->qhk', grad_heads[block], values_all)
        grads = probs * (dots - delta[block][..., None])
        grads_low = rounded(grads)
        query_part = jnp.einsum('qhk,khd->qhd', grads_low, keys_all) * scale
        key_acc = key_acc + jnp.einsum('qhk,qhd->khd', grads_low, queries[block]) * scale
        value_acc = value_acc + jnp.einsum('qhk,qhd->khd', rounded(probs), grad_heads[block])
        return (key_acc, value_acc), query_part.astype(jnp.bfloat16).reshape(TOK_DEV, D)

    zeros = jnp.zeros((TOKENS, HEADS, HD), jnp.float32)
    (key_acc, value_acc), query_grad = lax.scan(backward, (zeros, zeros), blocks)
    return (mixed, query_grad.reshape(TOKENS, D), key_acc.astype(jnp.bfloat16).reshape(TOKENS, D),
            value_acc.astype(jnp.bfloat16).reshape(TOKENS, D))
```

```python
import jax
import jax.numpy as jnp
from jax import lax
from jax.experimental import pallas as pl
from jax.experimental.pallas import tpu as pltpu
from jax.sharding import PartitionSpec as P

HD = 128
ROWS = 256
HEADS = 3
NQ = 4
NK = 8
QN = NQ * ROWS
KN = NK * ROWS
SCALE = HD ** (-0.5)
LOG2E = 1.4426950408889634
C2 = SCALE * LOG2E
NEG = -1e30
MESH = pl.DeviceIdType.MESH
f32 = jnp.float32
bf16 = jnp.bfloat16


def dot(a, b, left, right):
    return lax.dot_general(a, b, (((left,), (right,)), ((), ())), preferred_element_type=f32)


def slot_of(core, step):
    return core * 4 + (step + 3) % 4


def kernel(
    q_in, k_in, v_in, w_in, g_in, place, sinks, table,
    mixed_out, dq_out, dk_out, dv_out,
    qg, dog, kg, vg, wts, s_buf, kaug, qaug, ow, og, o_t, st, attn,
    o_send, o_recv, dq_send, dq_recv, sib_send, sib_recv, z_send, z_recv, own_kv, m_send, m_recv,
    local_sem, q_ss, q_rs, kv_ss, kv_rs, fw_ss, fw_rs, x_ss, x_rs, do_ss, do_rs, st_ss, st_rs,
    o_ss, o_rs, dq_ss, dq_rs, sg_ss, sg_rs, zg_ss, zg_rs, m_ss, m_rs,
):
    s = lax.axis_index("seq")
    x = lax.axis_index("head")
    c = lax.rem(s, 2)
    y = lax.rem(s // 2, 4)
    z = s // 8

    def y_peer(d):
        return {"seq": (z * 4 + lax.rem(y + d, 4)) * 2 + c}

    def z_peer(d):
        return {"seq": (lax.rem(z + d, 4) * 4 + y) * 2 + c}

    def x_peer(d):
        return {"head": lax.rem(x + d, 4)}

    sibling = {"seq": s + 1 - 2 * c}

    def remote(src, dst, send_sem, recv_sem, peer):
        return pltpu.make_async_remote_copy(
            src_ref=src, dst_ref=dst, send_sem=send_sem, recv_sem=recv_sem, device_id=peer, device_id_type=MESH
        )

    def cols(h):
        return pl.ds(h * HD, HD)

    local = [pltpu.make_async_copy(g_in, og.at[x], local_sem.at[0]), pltpu.make_async_copy(w_in, ow, local_sem.at[1])]
    for h in range(HEADS):
        local.append(pltpu.make_async_copy(q_in.at[:, cols(h)], qg.at[h, y], local_sem.at[2 + h]))
        local.append(pltpu.make_async_copy(k_in.at[:, cols(h)], kg.at[h, slot_of(0, 0)], local_sem.at[5 + h]))
        local.append(pltpu.make_async_copy(v_in.at[:, cols(h)], vg.at[h, slot_of(0, 0)], local_sem.at[8 + h]))
    for copy in local:
        copy.start()

    peers = [y_peer(1), y_peer(2), y_peer(3), z_peer(1), z_peer(2), z_peer(3), x_peer(1), x_peer(2), x_peer(3), sibling]
    barrier = pltpu.get_barrier_semaphore()
    for peer in peers:
        pl.semaphore_signal(barrier, inc=1, device_id=peer, device_id_type=MESH)
    pl.semaphore_wait(barrier, len(peers))

    x_copies = [remote(g_in, og.at[x], x_ss.at[d - 1], x_rs.at[d - 1], x_peer(d)) for d in (1, 2, 3)]
    q_copies, kv_copies, fw_copies = [], {}, {}
    for copy in x_copies:
        copy.start()
    for h in range(HEADS):
        q_copies.append([
            remote(q_in.at[:, cols(h)], qg.at[h, y], q_ss.at[h, d - 1], q_rs.at[h, d - 1], y_peer(d)) for d in (1, 3, 2)
        ])
    for n, (src, dst) in enumerate(((k_in, kg), (v_in, vg))):
        for h in range(HEADS):
            kv_copies[n, h] = [
                remote(
                    src.at[:, cols(h)], dst.at[h, slot_of(0, 4 - d)], kv_ss.at[n, h, d - 1], kv_rs.at[n, h, d - 1], z_peer(d)
                )
                for d in (1, 3, 2)
            ]
            fw_copies[n, h] = [
                remote(
                    src.at[:, cols(h)] if d == 0 else dst.at[h, slot_of(0, 4 - d)],
                    dst.at[h, slot_of(1, (4 - d) % 4)],
                    fw_ss.at[n, h, d], fw_rs.at[n, h, d], sibling,
                )
                for d in (0, 1, 3, 2)
            ]
    for h in range(HEADS):
        for a, b in zip(kv_copies[0, h], q_copies[h]):
            a.start()
            b.start()
        fw_copies[0, h][0].start()
    for h in range(HEADS):
        for a in kv_copies[1, h]:
            a.start()
        fw_copies[1, h][0].start()

    lane = lax.broadcasted_iota(jnp.int32, (1, HD), 1)
    q_spans = [place[(z * 4 + j) * 2 + c] for j in range(NQ)]
    row = lax.broadcasted_iota(jnp.int32, (ROWS, sinks.shape[1]), 0)
    ids = sinks[...]
    for core in range(2):
        for step in range(4):
            block = (lax.rem(z + step, 4) * 4 + y) * 2 + (c if core == 0 else 1 - c)
            span = place[block]
            bias = jnp.zeros((1, HD), f32)
            for j in range(NQ):
                barred = (1 - table[q_spans[j], span]).astype(f32) * NEG
                bias = bias + jnp.where(lane == j, barred, 0.0)
            sink = jnp.max(jnp.where(row + block * ROWS == ids, 1.0, 0.0), axis=1, keepdims=True)
            kaug[slot_of(core, step)] = jnp.where(sink > 0.5, 0.0, bias).astype(bf16)
    for j in range(NQ):
        qaug[j] = jnp.broadcast_to(jnp.where(lane == j, 1.0, 0.0), (ROWS, HD)).astype(bf16)

    def forward_keys(n, h):
        for a, b in zip(kv_copies[n, h], fw_copies[n, h][1:]):
            a.wait_recv()
            b.start()
        for b in fw_copies[n, h]:
            b.wait_recv()

    def scores(h):
        def one(j, carry):
            queries = jnp.concatenate([qg[h, j], qaug[j]], axis=1)
            half = pl.ds(pl.multiple_of(lax.rem(j, 2) * ROWS, ROWS), ROWS)
            mine = pl.ds(pl.multiple_of(j * ROWS, ROWS), ROWS)
            top = jnp.full((8, ROWS), -jnp.inf, f32)
            for i in range(NK):
                keys = jnp.concatenate([kg[h, i], kaug[i]], axis=1)
                t = dot(keys, queries, 1, 1)
                s_buf[pl.ds(i * ROWS, ROWS), half] = t
                top = jnp.maximum(top, jnp.max(t.reshape(ROWS // 8, 8, ROWS), axis=0))
            m = jnp.max(top, axis=0, keepdims=True) * C2
            total = jnp.zeros((8, ROWS), f32)
            for i in range(NK):
                w = jnp.exp2(s_buf[pl.ds(i * ROWS, ROWS), half] * C2 - m)
                wts[h, pl.ds(i * ROWS, ROWS), mine] = w.astype(bf16)
                total = total + jnp.sum(w.reshape(ROWS // 8, 8, ROWS), axis=0)
            st[h, y, pl.ds(j, 1), :] = m
            st[h, y, pl.ds(NQ + j, 1), :] = jnp.sum(total, axis=0, keepdims=True)
            return carry

        lax.fori_loop(0, NQ, one, 0, unroll=True)

    def weigh(h):
        for j in range(NQ):
            mine = pl.ds(j * ROWS, ROWS)
            o_t[h, :, mine] = dot(vg[h].reshape(KN, HD), wts[h, :, mine], 0, 0)

    def deltas(h):
        for j in range(NQ):
            prod = o_t[h, :, pl.ds(j * ROWS, ROWS)] * dog[h, j].astype(f32).T
            st[h, y, pl.ds(2 * NQ + j, 1), :] = jnp.sum(prod, axis=0, keepdims=True)

    def combine(h):
        ms = [st[h, g, pl.ds(0, NQ), :] for g in range(4)]
        top = jnp.maximum(jnp.maximum(ms[0], ms[1]), jnp.maximum(ms[2], ms[3]))
        es = [jnp.exp2(m - top) for m in ms]
        total = sum(e * st[h, g, pl.ds(NQ, NQ), :] for g, e in enumerate(es))
        summed = sum(e * st[h, g, pl.ds(2 * NQ, NQ), :] for g, e in enumerate(es))
        factor = jnp.exp2(st[h, y, pl.ds(0, NQ), :] - top) / total
        return factor, summed / total

    def as_row(a):
        return jnp.concatenate([a[j : j + 1] for j in range(NQ)], axis=1)

    for copy in local:
        copy.wait()
    for h in range(HEADS):
        for copy in q_copies[h]:
            copy.wait_recv()
        forward_keys(0, h)
        scores(h)

    for copy in x_copies:
        copy.wait_recv()
    do_copies = []
    for h in range(HEADS):
        d_attn = dot(og[...].reshape(ROWS, og.shape[2]), ow[cols(h), :], 1, 1)
        dog[h, y] = d_attn.astype(bf16)
        do_copies.append([
            remote(dog.at[h, y], dog.at[h, y], do_ss.at[h, d - 1], do_rs.at[h, d - 1], y_peer(d)) for d in (1, 3, 2)
        ])
        for copy in do_copies[h]:
            copy.start()

    for h in range(HEADS):
        forward_keys(1, h)
        weigh(h)

    st_copies = []
    for h in range(HEADS):
        for copy in do_copies[h]:
            copy.wait_recv()
        deltas(h)
        st_copies.append([
            remote(st.at[h, y], st.at[h, y], st_ss.at[h, d - 1], st_rs.at[h, d - 1], y_peer(d)) for d in (1, 3, 2)
        ])
        for copy in st_copies[h]:
            copy.start()

    factors, delta_rows, o_copies = [], [], []
    for h in range(HEADS):
        for copy in st_copies[h]:
            copy.wait_recv()
        factor, delta = combine(h)
        factors.append(as_row(factor))
        delta_rows.append(as_row(delta))
        for j in range(NQ):
            o_send[h, j] = (o_t[h, :, pl.ds(j * ROWS, ROWS)] * factor[j : j + 1]).T.astype(bf16)
        o_copies.append([
            remote(o_send.at[h, lax.rem(y + d, 4)], o_recv.at[h, d - 1], o_ss.at[h, d - 1], o_rs.at[h, d - 1], y_peer(d))
            for d in (1, 3, 2)
        ])
        for copy in o_copies[h]:
            copy.start()

    sg_copies, zg_copies, dq_copies = {}, {}, []

    def backward(h):
        factor, delta = factors[h], delta_rows[h]
        queries = qg[h].reshape(QN, HD)
        cots = dog[h].reshape(QN, HD)
        dq = jnp.zeros((HD, QN), f32)
        for t, first in enumerate((4, 6, 0, 2)):
            rows = pl.ds(first * ROWS, 2 * ROWS)
            keys = kg[h, pl.ds(first, 2)].reshape(2 * ROWS, HD)
            values = vg[h, pl.ds(first, 2)].reshape(2 * ROWS, HD)
            dots = dot(values, cots, 1, 1)
            probs = wts[h, rows, :].astype(f32) * factor
            grads = (probs * (dots - delta)).astype(bf16)
            dv = dot(probs.astype(bf16), cots, 1, 0)
            dk = dot(grads, queries, 1, 0) * SCALE
            dq = dq + dot(keys, grads, 0, 0)
            if first >= 4:
                for i in range(2):
                    sib_send[h, first - 4 + i, 0] = dk[i * ROWS : (i + 1) * ROWS].astype(bf16)
                    sib_send[h, first - 4 + i, 1] = dv[i * ROWS : (i + 1) * ROWS].astype(bf16)
                part = pl.ds(first - 4, 2)
                sg_copies[h, t] = remote(
                    sib_send.at[h, part], sib_recv.at[h, part], sg_ss.at[h, t], sg_rs.at[h, t], sibling
                )
                sg_copies[h, t].start()
            else:
                sg_copies[h, t - 2].wait_recv()
                for i in range(2):
                    slot = first + i
                    step = (slot + 1) % 4
                    for n, grad in enumerate((dk, dv)):
                        both = grad[i * ROWS : (i + 1) * ROWS] + sib_recv[h, slot, n].astype(f32)
                        if step == 0:
                            own_kv[h, n] = both
                        else:
                            z_send[h, step - 1, n] = both.astype(bf16)
                    if step != 0:
                        zg_copies[h, step] = remote(
                            z_send.at[h, step - 1], z_recv.at[h, step - 1], zg_ss.at[h, step - 1], zg_rs.at[h, step - 1],
                            z_peer(step),
                        )
                        zg_copies[h, step].start()
        for j in range(NQ):
            dq_send[h, j] = (dq[:, j * ROWS : (j + 1) * ROWS] * SCALE).T.astype(bf16)
        dq_copies.append([
            remote(dq_send.at[h, lax.rem(y + d, 4)], dq_recv.at[h, d - 1], dq_ss.at[h, d - 1], dq_rs.at[h, d - 1], y_peer(d))
            for d in (1, 3, 2)
        ])
        for copy in dq_copies[h]:
            copy.start()

    def finish(h):
        for copy in dq_copies[h]:
            copy.wait_recv()
        dq = dq_send[h, y].astype(f32)
        for i in range(3):
            dq = dq + dq_recv[h, i].astype(f32)
        dq_out[:, cols(h)] = dq.astype(bf16)
        for step in (1, 2, 3):
            zg_copies[h, step].wait_recv()
        for n, out in enumerate((dk_out, dv_out)):
            total = own_kv[h, n]
            for i in range(3):
                total = total + z_recv[h, i, n].astype(f32)
            out[:, cols(h)] = total.astype(bf16)

    backward(0)
    backward(1)

    for h in range(HEADS):
        for copy in o_copies[h]:
            copy.wait_recv()
        total = o_send[h, y].astype(f32)
        for i in range(3):
            total = total + o_recv[h, i].astype(f32)
        attn[:, cols(h)] = total.astype(bf16)
    m_send[...] = dot(attn[...], ow[...], 1, 0).astype(bf16).reshape(m_send.shape)
    m_copies = [
        remote(m_send.at[lax.rem(x + d, 4)], m_recv.at[d - 1], m_ss.at[d - 1], m_rs.at[d - 1], x_peer(d)) for d in (1, 3, 2)
    ]
    for copy in m_copies:
        copy.start()

    backward(2)
    finish(0)
    finish(1)
    for copy in m_copies:
        copy.wait_recv()
    mixed = m_send[x].astype(f32)
    for i in range(3):
        mixed = mixed + m_recv[i].astype(f32)
    mixed_out[...] = mixed.astype(bf16)
    finish(2)

    for copy in x_copies + m_copies:
        copy.wait_send()
    for group in q_copies + do_copies + st_copies + o_copies + dq_copies + list(kv_copies.values()) + list(fw_copies.values()):
        for copy in group:
            copy.wait_send()
    for copy in list(sg_copies.values()) + list(zg_copies.values()):
        copy.wait_send()


def on_device(
    query_states, key_states, value_states, out_weight, out_grad, placement, sink_ids, span_mask
):
    width = out_weight.shape[1]
    part = out_grad.shape[0]
    vmem = pl.BlockSpec(memory_space=pltpu.VMEM)
    smem = pl.BlockSpec(memory_space=pltpu.SMEM)
    hbm = pl.BlockSpec(memory_space=pl.ANY)
    own = (ROWS, HEADS * HD)

    def sem(*shape):
        return pltpu.SemaphoreType.DMA(shape)

    scratch = [
        pltpu.VMEM((HEADS, NQ, ROWS, HD), bf16),
        pltpu.VMEM((HEADS, NQ, ROWS, HD), bf16),
        pltpu.VMEM((HEADS, NK, ROWS, HD), bf16),
        pltpu.VMEM((HEADS, NK, ROWS, HD), bf16),
        pltpu.VMEM((HEADS, KN, QN), bf16),
        pltpu.VMEM((KN, 2 * ROWS), f32),
        pltpu.VMEM((NK, ROWS, HD), bf16),
        pltpu.VMEM((NQ, ROWS, HD), bf16),
        pltpu.VMEM((HEADS * HD, width), bf16),
        pltpu.VMEM((4, part, width), bf16),
        pltpu.VMEM((HEADS, HD, QN), f32),
        pltpu.VMEM((HEADS, 4, 16, ROWS), f32),
        pltpu.VMEM(own, bf16),
        pltpu.VMEM((HEADS, NQ, ROWS, HD), bf16),
        pltpu.VMEM((HEADS, 3, ROWS, HD), bf16),
        pltpu.VMEM((HEADS, NQ, ROWS, HD), bf16),
        pltpu.VMEM((HEADS, 3, ROWS, HD), bf16),
        pltpu.VMEM((HEADS, 4, 2, ROWS, HD), bf16),
        pltpu.VMEM((HEADS, 4, 2, ROWS, HD), bf16),
        pltpu.VMEM((HEADS, 3, 2, ROWS, HD), bf16),
        pltpu.VMEM((HEADS, 3, 2, ROWS, HD), bf16),
        pltpu.VMEM((HEADS, 2, ROWS, HD), f32),
        pltpu.VMEM((4, part, width), bf16),
        pltpu.VMEM((3, part, width), bf16),
        sem(11),
        sem(HEADS, 3), sem(HEADS, 3),
        sem(2, HEADS, 3), sem(2, HEADS, 3),
        sem(2, HEADS, 4), sem(2, HEADS, 4),
        sem(3), sem(3),
        sem(HEADS, 3), sem(HEADS, 3),
        sem(HEADS, 3), sem(HEADS, 3),
        sem(HEADS, 3), sem(HEADS, 3),
        sem(HEADS, 3), sem(HEADS, 3),
        sem(HEADS, 2), sem(HEADS, 2),
        sem(HEADS, 3), sem(HEADS, 3),
        sem(3), sem(3),
    ]
    return pl.pallas_call(
        kernel,
        out_shape=[jax.ShapeDtypeStruct((part, width), bf16)] + [jax.ShapeDtypeStruct(own, bf16)] * 3,
        in_specs=[hbm] * 5 + [smem, vmem, smem],
        out_specs=[vmem] * 4,
        scratch_shapes=scratch,
        compiler_params=pltpu.CompilerParams(
            collective_id=0, has_side_effects=True, vmem_limit_bytes=56 * 2**20
        ),
        name="attention",
    )(
        query_states, key_states, value_states, out_weight, out_grad,
        placement, sink_ids.reshape(1, -1), span_mask,
    )


def solution(mesh):
    in_specs = (
        P("seq", "head"),
        P("seq", "head"),
        P("seq", "head"),
        P("head", None),
        P(("seq", "head"), None),
        P(),
        P(),
        P(),
    )
    out_specs = (P(("seq", "head"), None), P("seq", "head"), P("seq", "head"), P("seq", "head"))
    return jax.shard_map(
        on_device, mesh=mesh, in_specs=in_specs, out_specs=out_specs, check_vma=False
    )
```

```python
import jax
import jax.numpy as jnp
from jax import lax
from jax.experimental import pallas as pl
from jax.experimental.pallas import tpu as pltpu
from jax.sharding import PartitionSpec as P

HD = 128
ROWS = 256
HEADS = 3
NQ = 4
NK = 8
QN = NQ * ROWS
KN = NK * ROWS
SCALE = HD ** (-0.5)
LOG2E = 1.4426950408889634
C2 = SCALE * LOG2E
NEG = -1e30
MESH = pl.DeviceIdType.MESH
f32 = jnp.float32
bf16 = jnp.bfloat16


def dot(a, b, left, right):
    return lax.dot_general(a, b, (((left,), (right,)), ((), ())), preferred_element_type=f32)


def slot_of(core, step):
    return core * 4 + (step + 3) % 4


def kernel(
    q_in, k_in, v_in, w_in, g_in, place, sinks, table,
    mixed_out, dq_out, dk_out, dv_out,
    qg, dog, kg, vg, wts, s_buf, kaug, qaug, ow, og, o_t, st, dl, attn,
    o_send, o_recv, dq_send, dq_recv, sib_send, sib_recv, z_send, z_recv, part_kv, m_send, m_recv,
    local_sem, q_ss, q_rs, kv_ss, kv_rs, fw_ss, fw_rs, x_ss, x_rs, do_ss, do_rs, st_ss, st_rs,
    d_ss, d_rs, o_ss, o_rs, dq_ss, dq_rs, sg_ss, sg_rs, zg_ss, zg_rs, m_ss, m_rs,
):
    s = lax.axis_index("seq")
    x = lax.axis_index("head")
    c = lax.rem(s, 2)
    y = lax.rem(s // 2, 4)
    z = s // 8

    def y_peer(d):
        return {"seq": (z * 4 + lax.rem(y + d, 4)) * 2 + c}

    def z_peer(d):
        return {"seq": (lax.rem(z + d, 4) * 4 + y) * 2 + c}

    def x_peer(d):
        return {"head": lax.rem(x + d, 4)}

    sibling = {"seq": s + 1 - 2 * c}

    def remote(src, dst, send_sem, recv_sem, peer):
        return pltpu.make_async_remote_copy(
            src_ref=src, dst_ref=dst, send_sem=send_sem, recv_sem=recv_sem, device_id=peer, device_id_type=MESH
        )

    def cols(h):
        return pl.ds(h * HD, HD)

    local = [pltpu.make_async_copy(g_in, og.at[x], local_sem.at[0]), pltpu.make_async_copy(w_in, ow, local_sem.at[1])]
    for h in range(HEADS):
        local.append(pltpu.make_async_copy(q_in.at[:, cols(h)], qg.at[h, y], local_sem.at[2 + h]))
        local.append(pltpu.make_async_copy(k_in.at[:, cols(h)], kg.at[h, slot_of(0, 0)], local_sem.at[5 + h]))
        local.append(pltpu.make_async_copy(v_in.at[:, cols(h)], vg.at[h, slot_of(0, 0)], local_sem.at[8 + h]))
    for copy in local:
        copy.start()

    peers = [y_peer(1), y_peer(2), y_peer(3), z_peer(1), z_peer(2), z_peer(3), x_peer(1), x_peer(2), x_peer(3), sibling]
    barrier = pltpu.get_barrier_semaphore()
    for peer in peers:
        pl.semaphore_signal(barrier, inc=1, device_id=peer, device_id_type=MESH)
    pl.semaphore_wait(barrier, len(peers))

    x_copies = [remote(g_in, og.at[x], x_ss.at[d - 1], x_rs.at[d - 1], x_peer(d)) for d in (1, 3, 2)]
    q_copies, kv_copies, fw_copies = [], {}, {}
    for copy in x_copies:
        copy.start()
    for h in range(HEADS):
        q_copies.append([
            remote(q_in.at[:, cols(h)], qg.at[h, y], q_ss.at[h, d - 1], q_rs.at[h, d - 1], y_peer(d)) for d in (1, 3, 2)
        ])
    for n, (src, dst) in enumerate(((k_in, kg), (v_in, vg))):
        for h in range(HEADS):
            kv_copies[n, h] = [
                remote(
                    src.at[:, cols(h)], dst.at[h, slot_of(0, 4 - d)], kv_ss.at[n, h, d - 1], kv_rs.at[n, h, d - 1], z_peer(d)
                )
                for d in (1, 3, 2)
            ]
            fw_copies[n, h] = [
                remote(
                    src.at[:, cols(h)] if d == 0 else dst.at[h, slot_of(0, 4 - d)],
                    dst.at[h, slot_of(1, (4 - d) % 4)],
                    fw_ss.at[n, h, d], fw_rs.at[n, h, d], sibling,
                )
                for d in (0, 1, 3, 2)
            ]
    for h in range(HEADS):
        for a, b in zip(kv_copies[0, h], q_copies[h]):
            a.start()
            b.start()
        fw_copies[0, h][0].start()
    for h in range(HEADS):
        for a in kv_copies[1, h]:
            a.start()
        fw_copies[1, h][0].start()

    lane = lax.broadcasted_iota(jnp.int32, (1, HD), 1)
    q_spans = [place[(z * 4 + j) * 2 + c] for j in range(NQ)]
    row = lax.broadcasted_iota(jnp.int32, (ROWS, sinks.shape[1]), 0)
    ids = sinks[...]
    for core in range(2):
        for step in range(4):
            block = (lax.rem(z + step, 4) * 4 + y) * 2 + (c if core == 0 else 1 - c)
            span = place[block]
            bias = jnp.zeros((1, HD), f32)
            for j in range(NQ):
                barred = (1 - table[q_spans[j], span]).astype(f32) * NEG
                bias = bias + jnp.where(lane == j, barred, 0.0)
            sink = jnp.max(jnp.where(row + block * ROWS == ids, 1.0, 0.0), axis=1, keepdims=True)
            kaug[slot_of(core, step)] = jnp.where(sink > 0.5, 0.0, bias).astype(bf16)
    for j in range(NQ):
        qaug[j] = jnp.broadcast_to(jnp.where(lane == j, 1.0, 0.0), (ROWS, HD)).astype(bf16)

    def forward(n, h):
        for a, b in zip(kv_copies[n, h], fw_copies[n, h][1:]):
            a.wait_recv()
            b.start()

    def await_forwarded(n, h):
        for b in fw_copies[n, h]:
            b.wait_recv()

    def share(buf, send_sems, recv_sems, h):
        copies = [
            remote(buf.at[h, y], buf.at[h, y], send_sems.at[h, d - 1], recv_sems.at[h, d - 1], y_peer(d)) for d in (1, 3, 2)
        ]
        for copy in copies:
            copy.start()
        return copies

    def await_all(copies):
        for copy in copies:
            copy.wait_recv()

    def scores(h):
        def one(j, carry):
            queries = jnp.concatenate([qg[h, j], qaug[j]], axis=1)
            half = pl.ds(pl.multiple_of(lax.rem(j, 2) * ROWS, ROWS), ROWS)
            mine = pl.ds(pl.multiple_of(j * ROWS, ROWS), ROWS)
            top = jnp.full((8, ROWS), -jnp.inf, f32)
            for i in range(NK):
                keys = jnp.concatenate([kg[h, i], kaug[i]], axis=1)
                t = dot(keys, queries, 1, 1)
                s_buf[pl.ds(i * ROWS, ROWS), half] = t
                top = jnp.maximum(top, jnp.max(t.reshape(ROWS // 8, 8, ROWS), axis=0))
            m = jnp.max(top, axis=0, keepdims=True) * C2
            total = jnp.zeros((8, ROWS), f32)
            for i in range(NK):
                w = jnp.exp2(s_buf[pl.ds(i * ROWS, ROWS), half] * C2 - m)
                wts[h, pl.ds(i * ROWS, ROWS), mine] = w.astype(bf16)
                total = total + jnp.sum(w.reshape(ROWS // 8, 8, ROWS), axis=0)
            st[h, y, pl.ds(j, 1), :] = m
            st[h, y, pl.ds(NQ + j, 1), :] = jnp.sum(total, axis=0, keepdims=True)
            return carry

        lax.fori_loop(0, NQ, one, 0, unroll=True)

    def weigh(h):
        for j in range(NQ // 2):
            mine = pl.ds(j * 2 * ROWS, 2 * ROWS)
            o_t[h, :, mine] = dot(vg[h].reshape(KN, HD), wts[h, :, mine], 0, 0)

    def combine(h):
        ms = [st[h, g, pl.ds(0, NQ), :] for g in range(4)]
        top = jnp.maximum(jnp.maximum(ms[0], ms[1]), jnp.maximum(ms[2], ms[3]))
        total = sum(jnp.exp2(m - top) * st[h, g, pl.ds(NQ, NQ), :] for g, m in enumerate(ms))
        return jnp.exp2(st[h, y, pl.ds(0, NQ), :] - top) / total

    def deltas(h, factor):
        for j in range(NQ):
            part = o_t[h, :, pl.ds(j * ROWS, ROWS)] * factor[j : j + 1]
            o_send[h, j] = part.T.astype(bf16)
            dl[h, y, pl.ds(j, 1), :] = jnp.sum(part * cotangents(j, h).astype(f32).T, axis=0, keepdims=True)

    def as_row(a):
        return jnp.concatenate([a[j : j + 1] for j in range(NQ)], axis=1)

    def send_cotangents(d):
        part = lax.rem(x + d, 4)
        d_attn = dot(og[part], ow[...], 1, 1).astype(bf16)
        for h in range(HEADS):
            dog[y, part, h] = d_attn[:, h * HD : (h + 1) * HD]
        for e in (1, 3, 2):
            copy = remote(dog.at[y, part], dog.at[y, part], do_ss.at[d, e - 1], do_rs.at[d, e - 1], y_peer(e))
            copy.start()
            do_copies.append(copy)

    def cotangents(j, h):
        return dog[j, :, h].reshape(ROWS, HD)

    def send_o(h):
        copies = [
            remote(o_send.at[h, lax.rem(y + d, 4)], o_recv.at[h, d - 1], o_ss.at[h, d - 1], o_rs.at[h, d - 1], y_peer(d))
            for d in (1, 3, 2)
        ]
        for copy in copies:
            copy.start()
        return copies

    sg_copies, zg_copies, dq_copies = {}, {}, []

    def to_sibling(n, h):
        sg_copies[n, h] = remote(sib_send.at[n, h], sib_recv.at[n, h], sg_ss.at[n, h], sg_rs.at[n, h], sibling)
        sg_copies[n, h].start()

    def relay(n, h):
        sg_copies[n, h].wait_recv()
        for step in (1, 3, 2, 0):
            slot = slot_of(0, step)
            total = part_kv[n, h, slot] + sib_recv[n, h, slot].astype(f32)
            if step == 0:
                part_kv[n, h, slot] = total
            else:
                z_send[n, h, step - 1] = total.astype(bf16)
                copy = remote(
                    z_send.at[n, h, step - 1], z_recv.at[n, h, step - 1], zg_ss.at[n, h, step - 1],
                    zg_rs.at[n, h, step - 1], z_peer(step),
                )
                copy.start()
                zg_copies[n, h, step] = copy

    def value_part(h):
        cots = dog[:, :, h].reshape(QN, HD)
        for first in (4, 6, 0, 2):
            rows = pl.ds(first * ROWS, 2 * ROWS)
            probs = (wts[h, rows, :].astype(f32) * factors[h]).astype(bf16)
            wts[h, rows, :] = probs
            dv = dot(probs, cots, 1, 0).reshape(2, ROWS, HD)
            if first >= 4:
                sib_send[0, h, pl.ds(first - 4, 2)] = dv.astype(bf16)
            else:
                part_kv[0, h, pl.ds(first, 2)] = dv
            if first == 6:
                to_sibling(0, h)

    def backward(h, then=()):
        await_all(d_copies[h])
        delta = as_row(sum(dl[h, g, pl.ds(0, NQ), :] for g in range(4)))
        queries = qg[h].reshape(QN, HD)
        cots = dog[:, :, h].reshape(QN, HD)
        dq = jnp.zeros((HD, QN), f32)
        for t, first in enumerate((4, 6, 0, 2)):
            rows = pl.ds(first * ROWS, 2 * ROWS)
            keys = kg[h, pl.ds(first, 2)].reshape(2 * ROWS, HD)
            values = vg[h, pl.ds(first, 2)].reshape(2 * ROWS, HD)
            dots = dot(values, cots, 1, 1)
            grads = (wts[h, rows, :].astype(f32) * (dots - delta)).astype(bf16)
            dk = (dot(grads, queries, 1, 0) * SCALE).reshape(2, ROWS, HD)
            dq = dq + dot(keys, grads, 0, 0)
            if first >= 4:
                sib_send[1, h, pl.ds(first - 4, 2)] = dk.astype(bf16)
            else:
                part_kv[1, h, pl.ds(first, 2)] = dk
            if first == 6:
                to_sibling(1, h)
            if t < len(then) and then[t] is not None:
                then[t]()
        for j in range(NQ):
            dq_send[h, j] = (dq[:, j * ROWS : (j + 1) * ROWS] * SCALE).T.astype(bf16)
        dq_copies.append([
            remote(dq_send.at[h, lax.rem(y + d, 4)], dq_recv.at[h, d - 1], dq_ss.at[h, d - 1], dq_rs.at[h, d - 1], y_peer(d))
            for d in (1, 3, 2)
        ])
        for copy in dq_copies[h]:
            copy.start()

    st_copies, do_copies, d_copies, o_copies, factors = [], [], [], [], []
    for copy in local:
        copy.wait()
    send_cotangents(0)
    for copy in x_copies[:2]:
        copy.wait_recv()
    send_cotangents(1)
    send_cotangents(3)
    forward(0, 0)
    await_forwarded(0, 0)
    await_all(q_copies[0])
    scores(0)
    st_copies.append(share(st, st_ss, st_rs, 0))
    forward(0, 1)

    x_copies[2].wait_recv()
    send_cotangents(2)

    for h in (1, 2):
        await_forwarded(0, h)
        await_all(q_copies[h])
        if h == 1:
            forward(0, 2)
        else:
            forward(1, 0)
        scores(h)
        st_copies.append(share(st, st_ss, st_rs, h))

    for h in range(HEADS):
        if h < 2:
            forward(1, h + 1)
        await_forwarded(1, h)
        weigh(h)
        await_all(st_copies[h])
        factor = combine(h)
        factors.append(as_row(factor))
        if h == 0:
            await_all(do_copies)
        deltas(h, factor)
        d_copies.append(share(dl, d_ss, d_rs, h))
        value_part(h)
        o_copies.append(send_o(h))
        if h > 0:
            relay(0, h - 1)

    def finish(h):
        for copy in dq_copies[h]:
            copy.wait_recv()
        dq = dq_send[h, y].astype(f32)
        for i in range(3):
            dq = dq + dq_recv[h, i].astype(f32)
        dq_out[:, cols(h)] = dq.astype(bf16)
        for n, out in enumerate((dv_out, dk_out)):
            total = part_kv[n, h, slot_of(0, 0)]
            for step in (1, 2, 3):
                zg_copies[n, h, step].wait_recv()
                total = total + z_recv[n, h, step - 1].astype(f32)
            out[:, cols(h)] = total.astype(bf16)

    m_copies = [
        remote(m_send.at[lax.rem(x + d, 4)], m_recv.at[d - 1], m_ss.at[d - 1], m_rs.at[d - 1], x_peer(d)) for d in (1, 3, 2)
    ]

    def project():
        for h in range(HEADS):
            await_all(o_copies[h])
            total = o_send[h, y].astype(f32)
            for i in range(3):
                total = total + o_recv[h, i].astype(f32)
            attn[:, cols(h)] = total.astype(bf16)
        m_send[...] = dot(attn[...], ow[...], 1, 0).astype(bf16).reshape(m_send.shape)
        for copy in m_copies:
            copy.start()

    backward(0, [lambda: relay(0, 2)])
    backward(1, [lambda: relay(1, 0), project])
    backward(2, [lambda: relay(1, 1)])
    relay(1, 2)
    finish(0)
    finish(1)
    for copy in m_copies:
        copy.wait_recv()
    mixed = m_send[x].astype(f32)
    for i in range(3):
        mixed = mixed + m_recv[i].astype(f32)
    mixed_out[...] = mixed.astype(bf16)
    finish(2)

    for copy in x_copies + m_copies:
        copy.wait_send()
    for group in q_copies + [do_copies] + st_copies + d_copies + o_copies + dq_copies + list(kv_copies.values()) + list(fw_copies.values()):
        for copy in group:
            copy.wait_send()
    for copy in list(sg_copies.values()) + list(zg_copies.values()):
        copy.wait_send()


def hand_over(*refs):
    for src, dst in zip(refs[:4], refs[4:]):
        dst[...] = src[...]


def on_device(
    query_states, key_states, value_states, out_weight, out_grad, placement, sink_ids, span_mask
):
    width = out_weight.shape[1]
    part = out_grad.shape[0]
    vmem = pl.BlockSpec(memory_space=pltpu.VMEM)
    smem = pl.BlockSpec(memory_space=pltpu.SMEM)
    hbm = pl.BlockSpec(memory_space=pl.ANY)
    own = (ROWS, HEADS * HD)

    def sem(*shape):
        return pltpu.SemaphoreType.DMA(shape)

    scratch = [
        pltpu.VMEM((HEADS, NQ, ROWS, HD), bf16),
        pltpu.VMEM((NQ, 4, HEADS, part, HD), bf16),
        pltpu.VMEM((HEADS, NK, ROWS, HD), bf16),
        pltpu.VMEM((HEADS, NK, ROWS, HD), bf16),
        pltpu.VMEM((HEADS, KN, QN), bf16),
        pltpu.VMEM((KN, 2 * ROWS), f32),
        pltpu.VMEM((NK, ROWS, HD), bf16),
        pltpu.VMEM((NQ, ROWS, HD), bf16),
        pltpu.VMEM((HEADS * HD, width), bf16),
        pltpu.VMEM((4, part, width), bf16),
        pltpu.VMEM((HEADS, HD, QN), f32),
        pltpu.VMEM((HEADS, 4, 8, ROWS), f32),
        pltpu.VMEM((HEADS, 4, 8, ROWS), f32),
        pltpu.VMEM(own, bf16),
        pltpu.VMEM((HEADS, NQ, ROWS, HD), bf16),
        pltpu.VMEM((HEADS, 3, ROWS, HD), bf16),
        pltpu.VMEM((HEADS, NQ, ROWS, HD), bf16),
        pltpu.VMEM((HEADS, 3, ROWS, HD), bf16),
        pltpu.VMEM((2, HEADS, 4, ROWS, HD), bf16),
        pltpu.VMEM((2, HEADS, 4, ROWS, HD), bf16),
        pltpu.VMEM((2, HEADS, 3, ROWS, HD), bf16),
        pltpu.VMEM((2, HEADS, 3, ROWS, HD), bf16),
        pltpu.VMEM((2, HEADS, 4, ROWS, HD), f32),
        pltpu.VMEM((4, part, width), bf16),
        pltpu.VMEM((3, part, width), bf16),
        sem(11),
        sem(HEADS, 3), sem(HEADS, 3),
        sem(2, HEADS, 3), sem(2, HEADS, 3),
        sem(2, HEADS, 4), sem(2, HEADS, 4),
        sem(3), sem(3),
        sem(4, 3), sem(4, 3),
        sem(HEADS, 3), sem(HEADS, 3),
        sem(HEADS, 3), sem(HEADS, 3),
        sem(HEADS, 3), sem(HEADS, 3),
        sem(HEADS, 3), sem(HEADS, 3),
        sem(2, HEADS), sem(2, HEADS),
        sem(2, HEADS, 3), sem(2, HEADS, 3),
        sem(3), sem(3),
    ]
    results = pl.pallas_call(
        kernel,
        out_shape=[pltpu.VMEM((part, width), bf16)] + [pltpu.VMEM(own, bf16)] * 3,
        in_specs=[hbm] * 5 + [smem, vmem, smem],
        out_specs=[vmem] * 4,
        scratch_shapes=scratch,
        compiler_params=pltpu.CompilerParams(
            collective_id=0, has_side_effects=True, vmem_limit_bytes=56 * 2**20
        ),
        name="attention",
    )(
        query_states, key_states, value_states, out_weight, out_grad,
        placement, sink_ids.reshape(1, -1), span_mask,
    )
    return pl.pallas_call(
        hand_over,
        out_shape=[jax.ShapeDtypeStruct(r.shape, r.dtype) for r in results],
        in_specs=[vmem] * 4,
        out_specs=[vmem] * 4,
        name="hand_over",
    )(*[pltpu.with_memory_space_constraint(r, pltpu.VMEM) for r in results])


def solution(mesh):
    in_specs = (
        P("seq", "head"),
        P("seq", "head"),
        P("seq", "head"),
        P("head", None),
        P(("seq", "head"), None),
        P(),
        P(),
        P(),
    )
    out_specs = (P(("seq", "head"), None), P("seq", "head"), P("seq", "head"), P("seq", "head"))
    return jax.shard_map(
        on_device, mesh=mesh, in_specs=in_specs, out_specs=out_specs, check_vma=False
    )
```

```python
import jax
import jax.numpy as jnp
from jax import lax
from jax.experimental import pallas as pl
from jax.experimental.pallas import tpu as pltpu
from jax.sharding import PartitionSpec as P

HD = 128
ROWS = 256
HEADS = 3
NQ = 4
NK = 8
QN = NQ * ROWS
KN = NK * ROWS
SCALE = HD ** (-0.5)
LOG2E = 1.4426950408889634
C2 = SCALE * LOG2E
NEG = -1e30
MESH = pl.DeviceIdType.MESH
f32 = jnp.float32
bf16 = jnp.bfloat16


def dot(a, b, left, right):
    return lax.dot_general(a, b, (((left,), (right,)), ((), ())), preferred_element_type=f32)


def slot_of(core, step):
    return core * 4 + (step + 3) % 4


def kernel(
    q_in, k_in, v_in, w_in, g_in, place, sinks, table,
    mixed_out, dq_out, dk_out, dv_out,
    qg, dog, cot, kg, vg, wts, s_buf, kaug, qaug, ow, og, o_t, st, dl, attn,
    o_send, o_recv, dq_send, dq_recv, sib_send, sib_recv, z_send, z_recv, part_kv, m_send, m_recv,
    local_sem, q_ss, q_rs, kv_ss, kv_rs, fw_ss, fw_rs, x_ss, x_rs, do_ss, do_rs, st_ss, st_rs,
    d_ss, d_rs, o_ss, o_rs, dq_ss, dq_rs, sg_ss, sg_rs, zg_ss, zg_rs, m_ss, m_rs,
):
    part = g_in.shape[0]
    s = lax.axis_index("seq")
    x = lax.axis_index("head")
    c = lax.rem(s, 2)
    y = lax.rem(s // 2, 4)
    z = s // 8

    def y_peer(d):
        return {"seq": (z * 4 + lax.rem(y + d, 4)) * 2 + c}

    def z_peer(d):
        return {"seq": (lax.rem(z + d, 4) * 4 + y) * 2 + c}

    def x_peer(d):
        return {"head": lax.rem(x + d, 4)}

    sibling = {"seq": s + 1 - 2 * c}

    def remote(src, dst, send_sem, recv_sem, peer):
        return pltpu.make_async_remote_copy(
            src_ref=src, dst_ref=dst, send_sem=send_sem, recv_sem=recv_sem, device_id=peer, device_id_type=MESH
        )

    def cols(h):
        return pl.ds(h * HD, HD)

    local = [pltpu.make_async_copy(g_in, og.at[x], local_sem.at[0]), pltpu.make_async_copy(w_in, ow, local_sem.at[1])]
    for h in range(HEADS):
        local.append(pltpu.make_async_copy(q_in.at[:, cols(h)], qg.at[h, y], local_sem.at[2 + h]))
        local.append(pltpu.make_async_copy(k_in.at[:, cols(h)], kg.at[h, slot_of(0, 0)], local_sem.at[5 + h]))
        local.append(pltpu.make_async_copy(v_in.at[:, cols(h)], vg.at[h, slot_of(0, 0)], local_sem.at[8 + h]))
    for copy in local:
        copy.start()

    peers = [y_peer(1), y_peer(2), y_peer(3), z_peer(1), z_peer(2), z_peer(3), x_peer(1), x_peer(2), x_peer(3), sibling]
    barrier = pltpu.get_barrier_semaphore()
    for peer in peers:
        pl.semaphore_signal(barrier, inc=1, device_id=peer, device_id_type=MESH)
    for copy in local:
        copy.wait()
    pl.semaphore_wait(barrier, len(peers))

    x_copies = [remote(og.at[x], og.at[x], x_ss.at[d - 1], x_rs.at[d - 1], x_peer(d)) for d in (1, 3, 2)]
    q_copies, kv_copies, fw_copies = [], {}, {}
    for copy in x_copies:
        copy.start()
    for h in range(HEADS):
        q_copies.append([
            remote(qg.at[h, y], qg.at[h, y], q_ss.at[h, d - 1], q_rs.at[h, d - 1], y_peer(d)) for d in (1, 3, 2)
        ])
    for n, dst in enumerate((kg, vg)):
        for h in range(HEADS):
            kv_copies[n, h] = [
                remote(
                    dst.at[h, slot_of(0, 0)], dst.at[h, slot_of(0, 4 - d)], kv_ss.at[n, h, d - 1], kv_rs.at[n, h, d - 1], z_peer(d)
                )
                for d in (1, 3, 2)
            ]
            fw_copies[n, h] = [
                remote(
                    dst.at[h, slot_of(0, (4 - d) % 4)],
                    dst.at[h, slot_of(1, (4 - d) % 4)],
                    fw_ss.at[n, h, d], fw_rs.at[n, h, d], sibling,
                )
                for d in (0, 1, 3, 2)
            ]
    for h in range(HEADS):
        for a, b in zip(kv_copies[0, h], q_copies[h]):
            a.start()
            b.start()
        fw_copies[0, h][0].start()
    for h in range(HEADS):
        for a in kv_copies[1, h]:
            a.start()
        fw_copies[1, h][0].start()

    lane = lax.broadcasted_iota(jnp.int32, (1, HD), 1)
    q_spans = [place[(z * 4 + j) * 2 + c] for j in range(NQ)]
    row = lax.broadcasted_iota(jnp.int32, (ROWS, sinks.shape[1]), 0)
    ids = sinks[...]
    for core in range(2):
        for step in range(4):
            block = (lax.rem(z + step, 4) * 4 + y) * 2 + (c if core == 0 else 1 - c)
            span = place[block]
            bias = jnp.zeros((1, HD), f32)
            for j in range(NQ):
                barred = (1 - table[q_spans[j], span]).astype(f32) * NEG
                bias = bias + jnp.where(lane == j, barred, 0.0)
            sink = jnp.max(jnp.where(row + block * ROWS == ids, 1.0, 0.0), axis=1, keepdims=True)
            kaug[slot_of(core, step)] = jnp.where(sink > 0.5, 0.0, bias).astype(bf16)
    for j in range(NQ):
        qaug[j] = jnp.broadcast_to(jnp.where(lane == j, 1.0, 0.0), (ROWS, HD)).astype(bf16)

    def forward(n, h):
        for a, b in zip(kv_copies[n, h], fw_copies[n, h][1:]):
            a.wait_recv()
            b.start()

    def await_forwarded(n, h):
        for b in fw_copies[n, h]:
            b.wait_recv()

    def share(buf, send_sems, recv_sems, h):
        copies = [
            remote(buf.at[h, y], buf.at[h, y], send_sems.at[h, d - 1], recv_sems.at[h, d - 1], y_peer(d)) for d in (1, 3, 2)
        ]
        for copy in copies:
            copy.start()
        return copies

    def await_all(copies):
        for copy in copies:
            copy.wait_recv()

    def scores(h):
        def one(j, carry):
            queries = jnp.concatenate([qg[h, j], qaug[j]], axis=1)
            half = pl.ds(pl.multiple_of(lax.rem(j, 2) * ROWS, ROWS), ROWS)
            mine = pl.ds(pl.multiple_of(j * ROWS, ROWS), ROWS)
            top = jnp.full((8, ROWS), -jnp.inf, f32)
            for i in range(NK):
                keys = jnp.concatenate([kg[h, i], kaug[i]], axis=1)
                t = dot(keys, queries, 1, 1)
                s_buf[pl.ds(i * ROWS, ROWS), half] = t
                top = jnp.maximum(top, jnp.max(t.reshape(ROWS // 8, 8, ROWS), axis=0))
            m = jnp.max(top, axis=0, keepdims=True) * C2
            total = jnp.zeros((8, ROWS), f32)
            for i in range(NK):
                w = jnp.exp2(s_buf[pl.ds(i * ROWS, ROWS), half] * C2 - m)
                wts[h, pl.ds(i * ROWS, ROWS), mine] = w.astype(bf16)
                total = total + jnp.sum(w.reshape(ROWS // 8, 8, ROWS), axis=0)
            st[h, y, pl.ds(j, 1), :] = m
            st[h, y, pl.ds(NQ + j, 1), :] = jnp.sum(total, axis=0, keepdims=True)
            return carry

        lax.fori_loop(0, NQ, one, 0, unroll=True)

    def weigh(h):
        for j in range(NQ // 2):
            mine = pl.ds(j * 2 * ROWS, 2 * ROWS)
            o_t[h, :, mine] = dot(vg[h].reshape(KN, HD), wts[h, :, mine], 0, 0)

    def combine(h):
        ms = [st[h, g, pl.ds(0, NQ), :] for g in range(4)]
        top = jnp.maximum(jnp.maximum(ms[0], ms[1]), jnp.maximum(ms[2], ms[3]))
        total = sum(jnp.exp2(m - top) * st[h, g, pl.ds(NQ, NQ), :] for g, m in enumerate(ms))
        return jnp.exp2(st[h, y, pl.ds(0, NQ), :] - top) / total

    def deltas(h, factor):
        for j in range(NQ):
            part = o_t[h, :, pl.ds(j * ROWS, ROWS)] * factor[j : j + 1]
            o_send[h, j] = part.T.astype(bf16)
            dl[h, y, pl.ds(j, 1), :] = jnp.sum(part * cot[h, pl.ds(j * ROWS, ROWS)].astype(f32).T, axis=0, keepdims=True)

    def as_row(a):
        return jnp.concatenate([a[j : j + 1] for j in range(NQ)], axis=1)

    def send_cotangents(n):
        groups = (3, 0, 1) if n == 0 else (2,)
        grad = jnp.concatenate([og[lax.rem(x + d, 4)] for d in groups], axis=0)
        here = pl.ds(0, 3 * part) if n == 0 else pl.ds(3 * part, part)
        d_attn = dot(grad, ow[...], 1, 1).astype(bf16)
        for h in range(HEADS):
            dog[h, y, here] = d_attn[:, h * HD : (h + 1) * HD]
            for e in (1, 3, 2):
                copy = remote(
                    dog.at[h, y, here], dog.at[h, y, here], do_ss.at[n, h, e - 1], do_rs.at[n, h, e - 1], y_peer(e)
                )
                copy.start()
                do_copies[h].append(copy)

    def order_cotangents(h):
        for j in range(NQ):
            for i in range(4):
                first = pl.multiple_of(lax.rem(i + 5 - x, 4) * part, part)
                cot[h, pl.ds(j * ROWS + i * part, part)] = dog[h, j, pl.ds(first, part)]

    def send_o(h):
        copies = [
            remote(o_send.at[h, lax.rem(y + d, 4)], o_recv.at[h, d - 1], o_ss.at[h, d - 1], o_rs.at[h, d - 1], y_peer(d))
            for d in (1, 3, 2)
        ]
        for copy in copies:
            copy.start()
        return copies

    sg_copies, zg_copies, dq_copies = {}, {}, []

    def to_sibling(n, h):
        sg_copies[n, h] = remote(sib_send.at[n, h], sib_recv.at[n, h], sg_ss.at[n, h], sg_rs.at[n, h], sibling)
        sg_copies[n, h].start()

    def relay(n, h):
        sg_copies[n, h].wait_recv()
        for step in (1, 3, 2, 0):
            slot = slot_of(0, step)
            total = part_kv[n, h, slot] + sib_recv[n, h, slot].astype(f32)
            if step == 0:
                part_kv[n, h, slot] = total
            else:
                z_send[n, h, step - 1] = total.astype(bf16)
                copy = remote(
                    z_send.at[n, h, step - 1], z_recv.at[n, h, step - 1], zg_ss.at[n, h, step - 1],
                    zg_rs.at[n, h, step - 1], z_peer(step),
                )
                copy.start()
                zg_copies[n, h, step] = copy

    def value_part(h):
        cots = cot[h]
        for first in (4, 6, 0, 2):
            rows = pl.ds(first * ROWS, 2 * ROWS)
            probs = (wts[h, rows, :].astype(f32) * factors[h]).astype(bf16)
            wts[h, rows, :] = probs
            dv = dot(probs, cots, 1, 0).reshape(2, ROWS, HD)
            if first >= 4:
                sib_send[0, h, pl.ds(first - 4, 2)] = dv.astype(bf16)
            else:
                part_kv[0, h, pl.ds(first, 2)] = dv

    def backward(h, then=()):
        await_all(d_copies[h])
        delta = as_row(sum(dl[h, g, pl.ds(0, NQ), :] for g in range(4)))
        queries = qg[h].reshape(QN, HD)
        cots = cot[h]
        dq = jnp.zeros((HD, QN), f32)
        for t, first in enumerate((4, 6, 0, 2)):
            rows = pl.ds(first * ROWS, 2 * ROWS)
            keys = kg[h, pl.ds(first, 2)].reshape(2 * ROWS, HD)
            values = vg[h, pl.ds(first, 2)].reshape(2 * ROWS, HD)
            dots = dot(values, cots, 1, 1)
            grads = (wts[h, rows, :].astype(f32) * (dots - delta)).astype(bf16)
            dk = (dot(grads, queries, 1, 0) * SCALE).reshape(2, ROWS, HD)
            dq = dq + dot(keys, grads, 0, 0)
            if first >= 4:
                sib_send[1, h, pl.ds(first - 4, 2)] = dk.astype(bf16)
            else:
                part_kv[1, h, pl.ds(first, 2)] = dk
            if first == 6 and h == HEADS - 1:
                to_sibling(1, h)
        for j in range(NQ):
            dq_send[h, j] = (dq[:, j * ROWS : (j + 1) * ROWS] * SCALE).T.astype(bf16)
        dq_copies.append([
            remote(dq_send.at[h, lax.rem(y + d, 4)], dq_recv.at[h, d - 1], dq_ss.at[h, d - 1], dq_rs.at[h, d - 1], y_peer(d))
            for d in (1, 3, 2)
        ])
        for copy in dq_copies[h]:
            copy.start()
        if h < HEADS - 1:
            to_sibling(1, h)
        for step in then:
            step()

    st_copies, do_copies, d_copies, o_copies, factors = [], [[], [], []], [], [], []
    for copy in x_copies[:2]:
        copy.wait_recv()
    send_cotangents(0)
    forward(0, 0)
    await_forwarded(0, 0)
    await_all(q_copies[0])
    scores(0)
    st_copies.append(share(st, st_ss, st_rs, 0))
    forward(0, 1)

    x_copies[2].wait_recv()
    send_cotangents(1)

    for h in (1, 2):
        await_forwarded(0, h)
        await_all(q_copies[h])
        if h == 1:
            forward(0, 2)
        else:
            forward(1, 0)
        scores(h)
        st_copies.append(share(st, st_ss, st_rs, h))

    for h in range(HEADS):
        if h < 2:
            forward(1, h + 1)
        await_forwarded(1, h)
        await_all(st_copies[h])
        await_all(do_copies[h])
        weigh(h)
        factor = combine(h)
        factors.append(as_row(factor))
        order_cotangents(h)
        deltas(h, factor)
        value_part(h)
        d_copies.append(share(dl, d_ss, d_rs, h))
        to_sibling(0, h)
        o_copies.append(send_o(h))
        if h > 0:
            relay(0, h - 1)

    def finish(h):
        for copy in dq_copies[h]:
            copy.wait_recv()
        dq = dq_send[h, y].astype(f32)
        for i in range(3):
            dq = dq + dq_recv[h, i].astype(f32)
        dq_out[:, cols(h)] = dq.astype(bf16)
        for n, out in enumerate((dv_out, dk_out)):
            total = part_kv[n, h, slot_of(0, 0)]
            for step in (1, 2, 3):
                zg_copies[n, h, step].wait_recv()
                total = total + z_recv[n, h, step - 1].astype(f32)
            out[:, cols(h)] = total.astype(bf16)

    m_copies = [
        remote(m_send.at[lax.rem(x + d, 4)], m_recv.at[d - 1], m_ss.at[d - 1], m_rs.at[d - 1], x_peer(d)) for d in (1, 3, 2)
    ]

    def project():
        for h in range(HEADS):
            await_all(o_copies[h])
            total = o_send[h, y].astype(f32)
            for i in range(3):
                total = total + o_recv[h, i].astype(f32)
            attn[:, cols(h)] = total.astype(bf16)
        m_send[...] = dot(attn[...], ow[...], 1, 0).astype(bf16).reshape(m_send.shape)
        for copy in m_copies:
            copy.start()

    backward(0, [lambda: relay(0, 2)])
    backward(1, [lambda: relay(1, 0), project])
    backward(2, [lambda: relay(1, 1)])
    relay(1, 2)
    finish(0)
    finish(1)
    for copy in m_copies:
        copy.wait_recv()
    mixed = m_send[x].astype(f32)
    for i in range(3):
        mixed = mixed + m_recv[i].astype(f32)
    mixed_out[...] = mixed.astype(bf16)
    finish(2)

    for copy in x_copies + m_copies:
        copy.wait_send()
    for group in q_copies + do_copies + st_copies + d_copies + o_copies + dq_copies + list(kv_copies.values()) + list(fw_copies.values()):
        for copy in group:
            copy.wait_send()
    for copy in list(sg_copies.values()) + list(zg_copies.values()):
        copy.wait_send()


def hand_over(*refs):
    for src, dst in zip(refs[:4], refs[4:]):
        dst[...] = src[...]


def on_device(
    query_states, key_states, value_states, out_weight, out_grad, placement, sink_ids, span_mask
):
    width = out_weight.shape[1]
    part = out_grad.shape[0]
    vmem = pl.BlockSpec(memory_space=pltpu.VMEM)
    smem = pl.BlockSpec(memory_space=pltpu.SMEM)
    hbm = pl.BlockSpec(memory_space=pl.ANY)
    own = (ROWS, HEADS * HD)

    def sem(*shape):
        return pltpu.SemaphoreType.DMA(shape)

    scratch = [
        pltpu.VMEM((HEADS, NQ, ROWS, HD), bf16),
        pltpu.VMEM((HEADS, NQ, ROWS, HD), bf16),
        pltpu.VMEM((HEADS, QN, HD), bf16),
        pltpu.VMEM((HEADS, NK, ROWS, HD), bf16),
        pltpu.VMEM((HEADS, NK, ROWS, HD), bf16),
        pltpu.VMEM((HEADS, KN, QN), bf16),
        pltpu.VMEM((KN, 2 * ROWS), f32),
        pltpu.VMEM((NK, ROWS, HD), bf16),
        pltpu.VMEM((NQ, ROWS, HD), bf16),
        pltpu.VMEM((HEADS * HD, width), bf16),
        pltpu.VMEM((4, part, width), bf16),
        pltpu.VMEM((HEADS, HD, QN), f32),
        pltpu.VMEM((HEADS, 4, 8, ROWS), f32),
        pltpu.VMEM((HEADS, 4, 8, ROWS), f32),
        pltpu.VMEM(own, bf16),
        pltpu.VMEM((HEADS, NQ, ROWS, HD), bf16),
        pltpu.VMEM((HEADS, 3, ROWS, HD), bf16),
        pltpu.VMEM((HEADS, NQ, ROWS, HD), bf16),
        pltpu.VMEM((HEADS, 3, ROWS, HD), bf16),
        pltpu.VMEM((2, HEADS, 4, ROWS, HD), bf16),
        pltpu.VMEM((2, HEADS, 4, ROWS, HD), bf16),
        pltpu.VMEM((2, HEADS, 3, ROWS, HD), bf16),
        pltpu.VMEM((2, HEADS, 3, ROWS, HD), bf16),
        pltpu.VMEM((2, HEADS, 4, ROWS, HD), f32),
        pltpu.VMEM((4, part, width), bf16),
        pltpu.VMEM((3, part, width), bf16),
        sem(11),
        sem(HEADS, 3), sem(HEADS, 3),
        sem(2, HEADS, 3), sem(2, HEADS, 3),
        sem(2, HEADS, 4), sem(2, HEADS, 4),
        sem(3), sem(3),
        sem(2, HEADS, 3), sem(2, HEADS, 3),
        sem(HEADS, 3), sem(HEADS, 3),
        sem(HEADS, 3), sem(HEADS, 3),
        sem(HEADS, 3), sem(HEADS, 3),
        sem(HEADS, 3), sem(HEADS, 3),
        sem(2, HEADS), sem(2, HEADS),
        sem(2, HEADS, 3), sem(2, HEADS, 3),
        sem(3), sem(3),
    ]
    results = pl.pallas_call(
        kernel,
        out_shape=[pltpu.VMEM((part, width), bf16)] + [pltpu.VMEM(own, bf16)] * 3,
        in_specs=[hbm] * 5 + [smem, vmem, smem],
        out_specs=[vmem] * 4,
        scratch_shapes=scratch,
        compiler_params=pltpu.CompilerParams(
            collective_id=0, has_side_effects=True, vmem_limit_bytes=56 * 2**20
        ),
        name="attention",
    )(
        query_states, key_states, value_states, out_weight, out_grad,
        placement, sink_ids.reshape(1, -1), span_mask,
    )
    return pl.pallas_call(
        hand_over,
        out_shape=[jax.ShapeDtypeStruct(r.shape, r.dtype) for r in results],
        in_specs=[vmem] * 4,
        out_specs=[vmem] * 4,
        name="hand_over",
    )(*[pltpu.with_memory_space_constraint(r, pltpu.VMEM) for r in results])


def solution(mesh):
    in_specs = (
        P("seq", "head"),
        P("seq", "head"),
        P("seq", "head"),
        P("head", None),
        P(("seq", "head"), None),
        P(),
        P(),
        P(),
    )
    out_specs = (P(("seq", "head"), None), P("seq", "head"), P("seq", "head"), P("seq", "head"))
    return jax.shard_map(
        on_device, mesh=mesh, in_specs=in_specs, out_specs=out_specs, check_vma=False
    )
```

```python
import jax
import jax.numpy as jnp
from jax import lax
from jax.experimental import pallas as pl
from jax.experimental.pallas import tpu as pltpu
from jax.sharding import PartitionSpec as P

HD = 128
ROWS = 256
HEADS = 3
NQ = 4
NK = 8
QN = NQ * ROWS
KN = NK * ROWS
SCALE = HD ** (-0.5)
LOG2E = 1.4426950408889634
C2 = SCALE * LOG2E
NEG = -1e30
MESH = pl.DeviceIdType.MESH
f32 = jnp.float32
bf16 = jnp.bfloat16


def dot(a, b, left, right):
    return lax.dot_general(a, b, (((left,), (right,)), ((), ())), preferred_element_type=f32)


def slot_of(core, step):
    return core * 4 + (step + 3) % 4


def kernel(
    q_in, k_in, v_in, w_in, g_in, place, sinks, table,
    mixed_out, dq_out, dk_out, dv_out,
    qg, dog, cot, kg, vg, wts, s_buf, kaug, qaug, ow, og, o_t, st, dl, attn,
    o_send, o_recv, dq_send, dq_recv, sib_send, sib_recv, z_send, z_recv, part_kv, m_send, m_recv,
    local_sem, q_ss, q_rs, kv_ss, kv_rs, fw_ss, fw_rs, x_ss, x_rs, do_ss, do_rs, st_ss, st_rs,
    d_ss, d_rs, o_ss, o_rs, dq_ss, dq_rs, sg_ss, sg_rs, zg_ss, zg_rs, m_ss, m_rs,
):
    part = g_in.shape[0]
    s = lax.axis_index("seq")
    x = lax.axis_index("head")
    c = lax.rem(s, 2)
    y = lax.rem(s // 2, 4)
    z = s // 8

    def y_peer(d):
        return {"seq": (z * 4 + lax.rem(y + d, 4)) * 2 + c}

    def z_peer(d):
        return {"seq": (lax.rem(z + d, 4) * 4 + y) * 2 + c}

    def x_peer(d):
        return {"head": lax.rem(x + d, 4)}

    sibling = {"seq": s + 1 - 2 * c}

    def remote(src, dst, send_sem, recv_sem, peer):
        return pltpu.make_async_remote_copy(
            src_ref=src, dst_ref=dst, send_sem=send_sem, recv_sem=recv_sem, device_id=peer, device_id_type=MESH
        )

    def cols(h):
        return pl.ds(h * HD, HD)

    local = [pltpu.make_async_copy(g_in, og.at[x], local_sem.at[0]), pltpu.make_async_copy(w_in, ow, local_sem.at[1])]
    for h in range(HEADS):
        local.append(pltpu.make_async_copy(q_in.at[:, cols(h)], qg.at[h, y], local_sem.at[2 + h]))
        local.append(pltpu.make_async_copy(k_in.at[:, cols(h)], kg.at[h, slot_of(0, 0)], local_sem.at[5 + h]))
        local.append(pltpu.make_async_copy(v_in.at[:, cols(h)], vg.at[h, slot_of(0, 0)], local_sem.at[8 + h]))
    for copy in local:
        copy.start()

    peers = [y_peer(1), y_peer(2), y_peer(3), z_peer(1), z_peer(2), z_peer(3), x_peer(1), x_peer(2), x_peer(3), sibling]
    barrier = pltpu.get_barrier_semaphore()
    for peer in peers:
        pl.semaphore_signal(barrier, inc=1, device_id=peer, device_id_type=MESH)
    for copy in local:
        copy.wait()
    pl.semaphore_wait(barrier, len(peers))

    x_copies = [remote(og.at[x], og.at[x], x_ss.at[d - 1], x_rs.at[d - 1], x_peer(d)) for d in (1, 3, 2)]
    q_copies, kv_copies, fw_copies = [], {}, {}
    for copy in x_copies:
        copy.start()
    for h in range(HEADS):
        q_copies.append([
            remote(qg.at[h, y], qg.at[h, y], q_ss.at[h, d - 1], q_rs.at[h, d - 1], y_peer(d)) for d in (1, 3, 2)
        ])
    for n, dst in enumerate((kg, vg)):
        for h in range(HEADS):
            kv_copies[n, h] = [
                remote(
                    dst.at[h, slot_of(0, 0)], dst.at[h, slot_of(0, 4 - d)], kv_ss.at[n, h, d - 1], kv_rs.at[n, h, d - 1], z_peer(d)
                )
                for d in (1, 3, 2)
            ]
            fw_copies[n, h] = [
                remote(
                    dst.at[h, slot_of(0, (4 - d) % 4)],
                    dst.at[h, slot_of(1, (4 - d) % 4)],
                    fw_ss.at[n, h, d], fw_rs.at[n, h, d], sibling,
                )
                for d in (0, 1, 3, 2)
            ]
    for h in range(HEADS):
        for a, b in zip(kv_copies[0, h], q_copies[h]):
            a.start()
            b.start()
        fw_copies[0, h][0].start()
    for h in range(HEADS):
        for a in kv_copies[1, h]:
            a.start()
        fw_copies[1, h][0].start()

    lane = lax.broadcasted_iota(jnp.int32, (1, HD), 1)
    q_spans = [place[(z * 4 + j) * 2 + c] for j in range(NQ)]
    row = lax.broadcasted_iota(jnp.int32, (ROWS, sinks.shape[1]), 0)
    ids = sinks[...]
    for core in range(2):
        for step in range(4):
            block = (lax.rem(z + step, 4) * 4 + y) * 2 + (c if core == 0 else 1 - c)
            span = place[block]
            bias = jnp.zeros((1, HD), f32)
            for j in range(NQ):
                barred = (1 - table[q_spans[j], span]).astype(f32) * NEG
                bias = bias + jnp.where(lane == j, barred, 0.0)
            sink = jnp.max(jnp.where(row + block * ROWS == ids, 1.0, 0.0), axis=1, keepdims=True)
            kaug[slot_of(core, step)] = jnp.where(sink > 0.5, 0.0, bias).astype(bf16)
    for j in range(NQ):
        qaug[j] = jnp.broadcast_to(jnp.where(lane == j, 1.0, 0.0), (ROWS, HD)).astype(bf16)

    def forward(n, h):
        for a, b in zip(kv_copies[n, h], fw_copies[n, h][1:]):
            a.wait_recv()
            b.start()

    def await_forwarded(n, h):
        for b in fw_copies[n, h]:
            b.wait_recv()

    def share(buf, send_sems, recv_sems, h):
        copies = [
            remote(buf.at[h, y], buf.at[h, y], send_sems.at[h, d - 1], recv_sems.at[h, d - 1], y_peer(d)) for d in (1, 3, 2)
        ]
        for copy in copies:
            copy.start()
        return copies

    def await_all(copies):
        for copy in copies:
            copy.wait_recv()

    def scores(h):
        def one(j, carry):
            queries = jnp.concatenate([qg[h, j], qaug[j]], axis=1)
            half = pl.ds(pl.multiple_of(lax.rem(j, 2) * ROWS, ROWS), ROWS)
            mine = pl.ds(pl.multiple_of(j * ROWS, ROWS), ROWS)
            top = jnp.full((8, ROWS), -jnp.inf, f32)
            for i in range(NK):
                keys = jnp.concatenate([kg[h, i], kaug[i]], axis=1)
                t = dot(keys, queries, 1, 1)
                s_buf[pl.ds(i * ROWS, ROWS), half] = t
                top = jnp.maximum(top, jnp.max(t.reshape(ROWS // 8, 8, ROWS), axis=0))
            m = jnp.max(top, axis=0, keepdims=True) * C2
            total = jnp.zeros((8, ROWS), f32)
            for i in range(NK):
                w = jnp.exp2(s_buf[pl.ds(i * ROWS, ROWS), half] * C2 - m)
                wts[h, pl.ds(i * ROWS, ROWS), mine] = w.astype(bf16)
                total = total + jnp.sum(w.reshape(ROWS // 8, 8, ROWS), axis=0)
            st[h, y, pl.ds(j, 1), :] = m
            st[h, y, pl.ds(NQ + j, 1), :] = jnp.sum(total, axis=0, keepdims=True)
            return carry

        lax.fori_loop(0, NQ, one, 0, unroll=True)

    def weigh(h):
        for j in range(NQ // 2):
            mine = pl.ds(j * 2 * ROWS, 2 * ROWS)
            o_t[h, :, mine] = dot(vg[h].reshape(KN, HD), wts[h, :, mine], 0, 0)

    def combine(h):
        ms = [st[h, g, pl.ds(0, NQ), :] for g in range(4)]
        top = jnp.maximum(jnp.maximum(ms[0], ms[1]), jnp.maximum(ms[2], ms[3]))
        total = sum(jnp.exp2(m - top) * st[h, g, pl.ds(NQ, NQ), :] for g, m in enumerate(ms))
        return jnp.exp2(st[h, y, pl.ds(0, NQ), :] - top) / total

    def deltas(h, factor):
        for j in range(NQ):
            part = o_t[h, :, pl.ds(j * ROWS, ROWS)] * factor[j : j + 1]
            o_send[h, j] = part.T.astype(bf16)
            dl[h, y, pl.ds(j, 1), :] = jnp.sum(part * cot[h, pl.ds(j * ROWS, ROWS)].astype(f32).T, axis=0, keepdims=True)

    def as_row(a):
        return jnp.concatenate([a[j : j + 1] for j in range(NQ)], axis=1)

    def send_cotangents(n):
        groups = (3, 0, 1) if n == 0 else (2,)
        grad = jnp.concatenate([og[lax.rem(x + d, 4)] for d in groups], axis=0)
        here = pl.ds(0, 3 * part) if n == 0 else pl.ds(3 * part, part)
        d_attn = dot(grad, ow[...], 1, 1).astype(bf16)
        for h in range(HEADS):
            dog[h, y, here] = d_attn[:, h * HD : (h + 1) * HD]
            for e in (1, 3, 2):
                copy = remote(
                    dog.at[h, y, here], dog.at[h, y, here], do_ss.at[n, h, e - 1], do_rs.at[n, h, e - 1], y_peer(e)
                )
                copy.start()
                do_copies[h].append(copy)

    def order_cotangents(h):
        for j in range(NQ):
            for i in range(4):
                first = pl.multiple_of(lax.rem(i + 5 - x, 4) * part, part)
                cot[h, pl.ds(j * ROWS + i * part, part)] = dog[h, j, pl.ds(first, part)]

    def send_o(h):
        copies = [
            remote(o_send.at[h, lax.rem(y + d, 4)], o_recv.at[h, d - 1], o_ss.at[h, d - 1], o_rs.at[h, d - 1], y_peer(d))
            for d in (1, 3, 2)
        ]
        for copy in copies:
            copy.start()
        return copies

    sg_copies, zg_copies, dq_copies = {}, {}, []

    def to_sibling(n, h):
        sg_copies[n, h] = remote(sib_send.at[n, h], sib_recv.at[n, h], sg_ss.at[n, h], sg_rs.at[n, h], sibling)
        sg_copies[n, h].start()

    def relay(n, h):
        sg_copies[n, h].wait_recv()
        for step in (1, 3, 2, 0):
            slot = slot_of(0, step)
            total = part_kv[n, h, slot] + sib_recv[n, h, slot].astype(f32)
            if step == 0:
                part_kv[n, h, slot] = total
            else:
                z_send[n, h, step - 1] = total.astype(bf16)
                copy = remote(
                    z_send.at[n, h, step - 1], z_recv.at[n, h, step - 1], zg_ss.at[n, h, step - 1],
                    zg_rs.at[n, h, step - 1], z_peer(step),
                )
                copy.start()
                zg_copies[n, h, step] = copy

    def value_part(h):
        cots = cot[h]
        for first in (4, 6, 0, 2):
            rows = pl.ds(first * ROWS, 2 * ROWS)
            probs = (wts[h, rows, :].astype(f32) * factors[h]).astype(bf16)
            wts[h, rows, :] = probs
            dv = dot(probs, cots, 1, 0).reshape(2, ROWS, HD)
            if first >= 4:
                sib_send[0, h, pl.ds(first - 4, 2)] = dv.astype(bf16)
            else:
                part_kv[0, h, pl.ds(first, 2)] = dv

    def backward(h, then=()):
        await_all(d_copies[h])
        delta = as_row(sum(dl[h, g, pl.ds(0, NQ), :] for g in range(4)))
        queries = qg[h].reshape(QN, HD)
        cots = cot[h]
        dq = jnp.zeros((HD, QN), f32)
        for t, first in enumerate((4, 6, 0, 2)):
            rows = pl.ds(first * ROWS, 2 * ROWS)
            keys = kg[h, pl.ds(first, 2)].reshape(2 * ROWS, HD)
            values = vg[h, pl.ds(first, 2)].reshape(2 * ROWS, HD)
            dots = dot(values, cots, 1, 1)
            grads = (wts[h, rows, :].astype(f32) * (dots - delta)).astype(bf16)
            dk = (dot(grads, queries, 1, 0) * SCALE).reshape(2, ROWS, HD)
            dq = dq + dot(keys, grads, 0, 0)
            if first >= 4:
                sib_send[1, h, pl.ds(first - 4, 2)] = dk.astype(bf16)
            else:
                part_kv[1, h, pl.ds(first, 2)] = dk
            if first == 6 and h == HEADS - 1:
                to_sibling(1, h)
                relay(1, h - 1)
        for j in range(NQ):
            dq_send[h, j] = (dq[:, j * ROWS : (j + 1) * ROWS] * SCALE).T.astype(bf16)
        dq_copies.append([
            remote(dq_send.at[h, lax.rem(y + d, 4)], dq_recv.at[h, d - 1], dq_ss.at[h, d - 1], dq_rs.at[h, d - 1], y_peer(d))
            for d in (1, 3, 2)
        ])
        for copy in dq_copies[h]:
            copy.start()
        if h < HEADS - 1:
            to_sibling(1, h)
        for step in then:
            step()

    st_copies, do_copies, d_copies, o_copies, factors = [], [[], [], []], [], [], []
    for copy in x_copies[:2]:
        copy.wait_recv()
    send_cotangents(0)
    forward(0, 0)
    await_forwarded(0, 0)
    await_all(q_copies[0])
    scores(0)
    st_copies.append(share(st, st_ss, st_rs, 0))
    forward(0, 1)

    x_copies[2].wait_recv()
    send_cotangents(1)

    for h in (1, 2):
        await_forwarded(0, h)
        await_all(q_copies[h])
        if h == 1:
            forward(0, 2)
        else:
            forward(1, 0)
        scores(h)
        st_copies.append(share(st, st_ss, st_rs, h))

    for h in range(HEADS):
        if h < 2:
            forward(1, h + 1)
        await_forwarded(1, h)
        await_all(st_copies[h])
        await_all(do_copies[h])
        weigh(h)
        factor = combine(h)
        factors.append(as_row(factor))
        order_cotangents(h)
        deltas(h, factor)
        value_part(h)
        d_copies.append(share(dl, d_ss, d_rs, h))
        to_sibling(0, h)
        o_copies.append(send_o(h))
        if h > 0:
            relay(0, h - 1)

    def finish(h):
        for copy in dq_copies[h]:
            copy.wait_recv()
        dq = dq_send[h, y].astype(f32)
        for i in range(3):
            dq = dq + dq_recv[h, i].astype(f32)
        dq_out[:, cols(h)] = dq.astype(bf16)
        for n, out in enumerate((dv_out, dk_out)):
            total = part_kv[n, h, slot_of(0, 0)]
            for step in (1, 2, 3):
                zg_copies[n, h, step].wait_recv()
                total = total + z_recv[n, h, step - 1].astype(f32)
            out[:, cols(h)] = total.astype(bf16)

    m_copies = [
        remote(m_send.at[lax.rem(x + d, 4)], m_recv.at[d - 1], m_ss.at[d - 1], m_rs.at[d - 1], x_peer(d)) for d in (1, 3, 2)
    ]

    def project():
        for h in range(HEADS):
            await_all(o_copies[h])
            total = o_send[h, y].astype(f32)
            for i in range(3):
                total = total + o_recv[h, i].astype(f32)
            attn[:, cols(h)] = total.astype(bf16)
        m_send[...] = dot(attn[...], ow[...], 1, 0).astype(bf16).reshape(m_send.shape)
        for copy in m_copies:
            copy.start()

    backward(0, [lambda: relay(0, 2)])
    backward(1, [lambda: relay(1, 0), project])
    backward(2)
    relay(1, 2)
    finish(0)
    finish(1)
    for copy in m_copies:
        copy.wait_recv()
    mixed = m_send[x].astype(f32)
    for i in range(3):
        mixed = mixed + m_recv[i].astype(f32)
    mixed_out[...] = mixed.astype(bf16)
    finish(2)

    for copy in x_copies + m_copies:
        copy.wait_send()
    for group in q_copies + do_copies + st_copies + d_copies + o_copies + dq_copies + list(kv_copies.values()) + list(fw_copies.values()):
        for copy in group:
            copy.wait_send()
    for copy in list(sg_copies.values()) + list(zg_copies.values()):
        copy.wait_send()


def hand_over(*refs):
    for src, dst in zip(refs[:4], refs[4:]):
        dst[...] = src[...]


def on_device(
    query_states, key_states, value_states, out_weight, out_grad, placement, sink_ids, span_mask
):
    width = out_weight.shape[1]
    part = out_grad.shape[0]
    vmem = pl.BlockSpec(memory_space=pltpu.VMEM)
    smem = pl.BlockSpec(memory_space=pltpu.SMEM)
    hbm = pl.BlockSpec(memory_space=pl.ANY)
    own = (ROWS, HEADS * HD)

    def sem(*shape):
        return pltpu.SemaphoreType.DMA(shape)

    scratch = [
        pltpu.VMEM((HEADS, NQ, ROWS, HD), bf16),
        pltpu.VMEM((HEADS, NQ, ROWS, HD), bf16),
        pltpu.VMEM((HEADS, QN, HD), bf16),
        pltpu.VMEM((HEADS, NK, ROWS, HD), bf16),
        pltpu.VMEM((HEADS, NK, ROWS, HD), bf16),
        pltpu.VMEM((HEADS, KN, QN), bf16),
        pltpu.VMEM((KN, 2 * ROWS), f32),
        pltpu.VMEM((NK, ROWS, HD), bf16),
        pltpu.VMEM((NQ, ROWS, HD), bf16),
        pltpu.VMEM((HEADS * HD, width), bf16),
        pltpu.VMEM((4, part, width), bf16),
        pltpu.VMEM((HEADS, HD, QN), f32),
        pltpu.VMEM((HEADS, 4, 8, ROWS), f32),
        pltpu.VMEM((HEADS, 4, 8, ROWS), f32),
        pltpu.VMEM(own, bf16),
        pltpu.VMEM((HEADS, NQ, ROWS, HD), bf16),
        pltpu.VMEM((HEADS, 3, ROWS, HD), bf16),
        pltpu.VMEM((HEADS, NQ, ROWS, HD), bf16),
        pltpu.VMEM((HEADS, 3, ROWS, HD), bf16),
        pltpu.VMEM((2, HEADS, 4, ROWS, HD), bf16),
        pltpu.VMEM((2, HEADS, 4, ROWS, HD), bf16),
        pltpu.VMEM((2, HEADS, 3, ROWS, HD), bf16),
        pltpu.VMEM((2, HEADS, 3, ROWS, HD), bf16),
        pltpu.VMEM((2, HEADS, 4, ROWS, HD), f32),
        pltpu.VMEM((4, part, width), bf16),
        pltpu.VMEM((3, part, width), bf16),
        sem(11),
        sem(HEADS, 3), sem(HEADS, 3),
        sem(2, HEADS, 3), sem(2, HEADS, 3),
        sem(2, HEADS, 4), sem(2, HEADS, 4),
        sem(3), sem(3),
        sem(2, HEADS, 3), sem(2, HEADS, 3),
        sem(HEADS, 3), sem(HEADS, 3),
        sem(HEADS, 3), sem(HEADS, 3),
        sem(HEADS, 3), sem(HEADS, 3),
        sem(HEADS, 3), sem(HEADS, 3),
        sem(2, HEADS), sem(2, HEADS),
        sem(2, HEADS, 3), sem(2, HEADS, 3),
        sem(3), sem(3),
    ]
    results = pl.pallas_call(
        kernel,
        out_shape=[pltpu.VMEM((part, width), bf16)] + [pltpu.VMEM(own, bf16)] * 3,
        in_specs=[hbm] * 5 + [smem, vmem, smem],
        out_specs=[vmem] * 4,
        scratch_shapes=scratch,
        compiler_params=pltpu.CompilerParams(
            collective_id=0, has_side_effects=True, vmem_limit_bytes=56 * 2**20
        ),
        name="attention",
    )(
        query_states, key_states, value_states, out_weight, out_grad,
        placement, sink_ids.reshape(1, -1), span_mask,
    )
    return pl.pallas_call(
        hand_over,
        out_shape=[jax.ShapeDtypeStruct(r.shape, r.dtype) for r in results],
        in_specs=[vmem] * 4,
        out_specs=[vmem] * 4,
        name="hand_over",
    )(*[pltpu.with_memory_space_constraint(r, pltpu.VMEM) for r in results])


def solution(mesh):
    in_specs = (
        P("seq", "head"),
        P("seq", "head"),
        P("seq", "head"),
        P("head", None),
        P(("seq", "head"), None),
        P(),
        P(),
        P(),
    )
    out_specs = (P(("seq", "head"), None), P("seq", "head"), P("seq", "head"), P("seq", "head"))
    return jax.shard_map(
        on_device, mesh=mesh, in_specs=in_specs, out_specs=out_specs, check_vma=False
    )
```
